32 devices in a mesh: lat: 4 (over x, core), lon: 8 (over z, y).
Axes of the slice: x: 2, y: 2, z: 4, core: 2. Of those that a mesh axis runs over, the one named last changes fastest.
Arguments:
- node_latents: bfloat16 [8192, 512], P(('lat', 'lon')), may hold values from -6 to 6
- edge_latents: bfloat16 [65536, 512], P(('lat', 'lon')), may hold values from -6 to 6
- edge_count: int32 [32], P(('lat', 'lon')), may hold values from 256 to 2048, as said below
- receiver: int32 [65536], P(('lat', 'lon')), may hold values from 0 to 255, as said below
- sender: int32 [65536], P(('lat', 'lon')), may hold values from 0 to 447, as said below
- halo_send: int32 [32, 4, 32], P(('lat', 'lon')), may hold values from 0 to 255
- far_send: int32 [32, 32, 2], P(('lat', 'lon')), may hold values from 0 to 255
- edge_weight_in: bfloat16 [1536, 512], replicated, may hold values from -0.15625 to 0.15625
- edge_bias: float32 [512], replicated, may hold values from -3 to 3
- edge_weight_out: bfloat16 [512, 512], replicated, may hold values from -0.25 to 0.25
- edge_gain: float32 [512], replicated, may hold values from 0.25 to 1.75
- node_weight_in: bfloat16 [1024, 512], replicated, may hold values from -0.1875 to 0.1875
- node_bias: float32 [512], replicated, may hold values from -3 to 3
- node_weight_out: bfloat16 [512, 512], replicated, may hold values from -0.25 to 0.25
- node_gain: float32 [512], replicated, may hold values from 0.25 to 1.75
- cot_nodes: bfloat16 [8192, 512], P(('lat', 'lon')), may hold values from -6 to 6
- cot_edges: bfloat16 [65536, 512], P(('lat', 'lon')), may hold values from -6 to 6
Outputs:
- node_out: bfloat16 [8192, 512], P(('lat', 'lon'))
- edge_out: bfloat16 [65536, 512], P(('lat', 'lon'))
- grad_nodes: bfloat16 [8192, 512], P(('lat', 'lon'))
- grad_edges: bfloat16 [65536, 512], P(('lat', 'lon'))
- grad_edge_weight_in: float32 [1536, 512], replicated
- grad_edge_bias: float32 [512], replicated
- grad_edge_weight_out: float32 [512, 512], replicated
- grad_edge_gain: float32 [512], replicated
- grad_node_weight_in: float32 [1024, 512], replicated
- grad_node_bias: float32 [512], replicated
- grad_node_weight_out: float32 [512, 512], replicated
- grad_node_gain: float32 [512], replicated
The draws below stay inside these ranges and needn't reach their ends.
Inputs may be any that keep to these rules, and one draw needn't show every extreme that they name: `edge_count`: edge slots of a device past its count are padding; some device has all 2048 slots live in every draw. `receiver`: nondecreasing within each device's 2048 edge slots. `sender`: rows below 256 are the device's own nodes, the next 128 the four neighbours' halo rows, the rest the 2 rows from each peer in device order; halo rows from a band that does not exist are never named.
All inputs are finite; a program needn't handle non-finite values.
Results may differ from the reference program's by a relative error of at most 0.017.
Values may be sent and summed in bfloat16 or wider, within the bound.
No kernel may reach another device: no remote copies, remote signals or barrier semaphores. Data moves between devices by JAX's collectives and lax.ppermute only.
A program may use at most 128 MiB of HBM per device.

```python
from functools import partial
import jax
import jax.numpy as jnp
from jax import lax

D = 512
NODE_DEV = 256
BORDER = 32
CAP = 2
EDGE_DEV = 2048
NODES = 8192
EDGES = 65536
BANDS = 4
TILES = 8
N_LAT = 4
N_LON = 8
DEVICES = 32


def live_counts(key):
    key_one, key_two = jax.random.split(key)
    level_draw = jax.random.randint(key_one, (DEVICES,), 0, 64, dtype=jnp.int32)
    least_count = EDGE_DEV // 8
    counts = least_count + level_draw * level_draw * (EDGE_DEV - least_count) // 3969
    busiest = jax.random.randint(key_two, (), 0, DEVICES, dtype=jnp.int32)
    return counts.at[busiest].set(EDGE_DEV).astype(jnp.int32)


def draw_edge_count(key, part):
    return live_counts(key)


def draw_receiver(key, part):
    counts = live_counts(key)
    key = jax.random.fold_in(key, 2)
    drawn = jax.random.randint(key, (DEVICES, EDGE_DEV), 0, NODE_DEV, dtype=jnp.int32)
    position = jnp.arange(EDGE_DEV, dtype=jnp.int32)[None, :]
    drawn = jnp.where(position < counts[:, None], drawn, NODE_DEV)
    ordered = jnp.minimum(jnp.sort(drawn, axis=1), NODE_DEV - 1)
    return ordered.reshape(-1).astype(jnp.int32)


def draw_sender(key, part):
    key = jax.random.fold_in(key, 3)
    keys = jax.random.split(key, 5)
    grid_shape = (DEVICES, EDGE_DEV)
    category = jax.random.randint(keys[0], grid_shape, 0, 20, dtype=jnp.int32)
    own_index = jax.random.randint(keys[1], grid_shape, 0, NODE_DEV, dtype=jnp.int32)
    direction = jax.random.randint(keys[2], grid_shape, 0, 4, dtype=jnp.int32)
    band_index = (jnp.arange(DEVICES, dtype=jnp.int32) // TILES)[:, None]
    direction = jnp.where((band_index == 0) & (direction == 0), 1, direction)
    direction = jnp.where((band_index == BANDS - 1) & (direction == 1), 0, direction)
    position = jax.random.randint(keys[3], grid_shape, 0, BORDER, dtype=jnp.int32)
    offset = jax.random.randint(keys[4], (DEVICES, 1), 0, DEVICES * CAP, dtype=jnp.int32)
    edge_position = jnp.arange(EDGE_DEV, dtype=jnp.int32)[None, :]
    far_slot = (edge_position + offset) % (DEVICES * CAP)
    picked = jnp.where(category < 10, own_index, jnp.where(category < 15, NODE_DEV + direction * BORDER + position, NODE_DEV + 4 * BORDER + far_slot))
    return picked.reshape(-1).astype(jnp.int32)


def place_ends(values, own_key, least, largest):
    extent = values.shape
    spot = [jax.random.randint(jax.random.fold_in(own_key, axis), (), 0, extent[axis]) for axis in range(len(extent))]
    values = values.at[tuple(spot)].set(least)
    longest = extent.index(max(extent))
    spot[longest] = (spot[longest] + 1) % extent[longest]
    return values.at[tuple(spot)].set(largest)


def block_scale(rng, dims, cuts, least, largest):
    level, own = 1.0, jax.random.fold_in(rng, 6)
    for dim, blocks in cuts:
        draws = jnp.exp(jax.random.uniform(jax.random.fold_in(own, dim), (blocks,), jnp.float32, least / len(cuts), largest / len(cuts)))
        level = level * jnp.repeat(draws, dims[dim] // blocks).reshape([-1 if axis == dim else 1 for axis in range(len(dims))])
    return level


def scatter_about(key, shape, width, reach, cuts=(), kind=jnp.bfloat16):
    array = jax.random.normal(key, shape, jnp.float32) * width
    if len(cuts) > 0:
        array = block_scale(key, shape, cuts, -0.22, 0.18) * array
    return jnp.clip(array, min=-reach, max=reach).astype(kind)


def setup_inputs(seed: int = 0) -> dict:
    streams_of = jax.random.split(jax.random.key(seed), 18)
    return {
        "node_latents": scatter_about(streams_of[0], (NODES, D), 1.0, 6.0, ((0, 32),)),
        "edge_latents": scatter_about(streams_of[1], (EDGES, D), 1.0, 6.0, ((0, 32),)),
        "edge_count": draw_edge_count(jax.random.fold_in(streams_of[17], 71), 0),
        "receiver": draw_receiver(jax.random.fold_in(streams_of[17], 71), 0),
        "sender": draw_sender(jax.random.fold_in(streams_of[17], 71), 0),
        "halo_send": place_ends(jax.random.randint(streams_of[5], (DEVICES, 4, BORDER), 0, NODE_DEV), jax.random.fold_in(streams_of[5], 1), 0, NODE_DEV - 1).astype(jnp.int32),
        "far_send": place_ends(jax.random.randint(streams_of[6], (DEVICES, DEVICES, CAP), 0, NODE_DEV), jax.random.fold_in(streams_of[6], 1), 0, NODE_DEV - 1).astype(jnp.int32),
        "edge_weight_in": scatter_about(streams_of[7], (3 * D, D), (3 * D) ** -0.5, 0.15625),
        "edge_bias": scatter_about(streams_of[8], (D,), 0.5, 3.0, (), jnp.float32),
        "edge_weight_out": scatter_about(streams_of[9], (D, D), D ** -0.5, 0.25),
        "edge_gain": jnp.clip(1.0 + 0.15 * jax.random.normal(streams_of[10], (D,), jnp.float32), 0.25, 1.75),
        "node_weight_in": scatter_about(streams_of[11], (2 * D, D), (2 * D) ** -0.5, 0.1875),
        "node_bias": scatter_about(streams_of[12], (D,), 0.5, 3.0, (), jnp.float32),
        "node_weight_out": scatter_about(streams_of[13], (D, D), D ** -0.5, 0.25),
        "node_gain": jnp.clip(1.0 + 0.15 * jax.random.normal(streams_of[14], (D,), jnp.float32), 0.25, 1.75),
        "cot_nodes": scatter_about(streams_of[15], (NODES, D), 1.0, 6.0, ((0, 32),)),
        "cot_edges": scatter_about(streams_of[16], (EDGES, D), 1.0, 6.0, ((0, 32),)),
    }


EPSILON = 1e-05

def layer_norm(values, gain_out):
    row_mean = lax.optimization_barrier(jnp.mean(values, axis=-1, keepdims=True))
    centered = values - row_mean
    variance = lax.optimization_barrier(jnp.mean(centered * centered, axis=-1, keepdims=True))
    return centered * lax.rsqrt(variance + EPSILON) * gain_out

def edge_update(params, edge_rows, sender_rows, receiver_rows, live_mask):
    weight_in, bias_in, weight_out, gain_out = params
    joined = jnp.concatenate([edge_rows, sender_rows, receiver_rows], axis=1)
    first_layer = jnp.dot(joined, weight_in, preferred_element_type=jnp.float32) + bias_in
    active = jax.nn.silu(first_layer).astype(jnp.bfloat16)
    second = jnp.dot(active, weight_out, preferred_element_type=jnp.float32)
    message = layer_norm(second, gain_out) * live_mask[:, None]
    updated = (edge_rows.astype(jnp.float32) + message).astype(jnp.bfloat16)
    return (updated, message)

def node_update(params, node_rows, gathered):
    weight_in, bias_in, weight_out, gain_out = params
    joined = jnp.concatenate([node_rows, gathered], axis=1)
    first_layer = jnp.dot(joined, weight_in, preferred_element_type=jnp.float32) + bias_in
    active = jax.nn.silu(first_layer).astype(jnp.bfloat16)
    second = jnp.dot(active, weight_out, preferred_element_type=jnp.float32)
    return (node_rows.astype(jnp.float32) + layer_norm(second, gain_out)).astype(jnp.bfloat16)

def global_senders(sender_block, halo_send, far_send):
    device_count = N_LAT * N_LON
    device_ids = jnp.arange(device_count, dtype=jnp.int32)[:, None]
    band_index = device_ids // N_LON
    tile_index = device_ids % N_LON
    halo_part = sender_block - NODE_DEV
    far_part = sender_block - NODE_DEV - 4 * BORDER
    direction = jnp.clip(halo_part // BORDER, 0, 3).astype(jnp.int32)
    position = jnp.clip(halo_part, 0, 4 * BORDER - 1) % BORDER
    band_step = jnp.where(direction == 0, -1, jnp.where(direction == 1, 1, 0))
    tile_step = jnp.where(direction == 2, -1, jnp.where(direction == 3, 1, 0))
    near_band = band_index + band_step
    near_tile = (tile_index + tile_step) % N_LON
    inside = (near_band >= 0) & (near_band < N_LAT)
    neighbour = (jnp.clip(near_band, 0, N_LAT - 1) * N_LON + near_tile).astype(jnp.int32)
    list_index = jnp.bitwise_xor(direction, 1).astype(jnp.int32)
    halo_row = halo_send[neighbour, list_index, position]
    halo_global = jnp.where(inside, neighbour * NODE_DEV + halo_row, NODES)
    peer_index = jnp.clip(far_part // CAP, 0, device_count - 1).astype(jnp.int32)
    slot_index = (jnp.clip(far_part, 0, device_count * CAP - 1) % CAP).astype(jnp.int32)
    far_row = far_send[peer_index, jnp.broadcast_to(device_ids, peer_index.shape), slot_index]
    far_global = peer_index * NODE_DEV + far_row
    own_global = device_ids * NODE_DEV + sender_block
    picked = jnp.where(sender_block < NODE_DEV, own_global, jnp.where(far_part < 0, halo_global, far_global))
    return picked.astype(jnp.int32)

def reference(node_latents, edge_latents, edge_count, receiver, sender, halo_send, far_send, edge_weight_in, edge_bias, edge_weight_out, edge_gain, node_weight_in, node_bias, node_weight_out, node_gain, cot_nodes, cot_edges):
    device_count = N_LAT * N_LON
    feature_width = node_latents.shape[1]
    sender_index = global_senders(sender.reshape(device_count, EDGE_DEV), halo_send, far_send)
    padded = jnp.concatenate([node_latents, jnp.zeros((1, feature_width), jnp.bfloat16)], axis=0)
    edge_params = (edge_weight_in, edge_bias, edge_weight_out, edge_gain)
    node_params = (node_weight_in, node_bias, node_weight_out, node_gain)

    def one_device(accumulated, device_item):
        param_sums, spread = accumulated
        own_nodes, own_edges, live_count, receiver_block, sender_block, node_cot, edge_cot_in = device_item
        live_mask = (lax.iota(jnp.int32, EDGE_DEV) < live_count).astype(jnp.float32)
        sent_rows = padded[sender_block]
        received_rows = own_nodes[receiver_block]
        (new_edges, message), edge_back = jax.vjp(partial(edge_update, live_mask=live_mask), edge_params, own_edges, sent_rows, received_rows)
        gathered = jax.ops.segment_sum(message, receiver_block, NODE_DEV, indices_are_sorted=True).astype(jnp.bfloat16)
        new_nodes, node_back = jax.vjp(node_update, node_params, own_nodes, gathered)
        node_grads, from_node, from_gathered = node_back(node_cot)
        edge_grads, edge_grad, from_send, from_receive = edge_back((edge_cot_in, from_gathered.astype(jnp.float32)[receiver_block]))
        local_totals = from_node.astype(jnp.float32) + jax.ops.segment_sum(from_receive.astype(jnp.float32), receiver_block, NODE_DEV, indices_are_sorted=True)
        spread = spread.at[sender_block].add(from_send.astype(jnp.float32))
        every_grad = tuple(edge_grads) + tuple(node_grads)
        param_sums = tuple((total + grad.astype(jnp.float32) for total, grad in zip(param_sums, every_grad)))
        return ((param_sums, spread), (new_nodes, new_edges, edge_grad, local_totals))
    every_param = edge_params + node_params
    start_sums = tuple((jnp.zeros(param.shape, jnp.float32) for param in every_param))
    start_spread = jnp.zeros((NODES + 1, feature_width), jnp.float32)
    device_items = (node_latents.reshape(device_count, NODE_DEV, feature_width), edge_latents.reshape(device_count, EDGE_DEV, feature_width), edge_count.astype(jnp.int32), receiver.reshape(device_count, EDGE_DEV), sender_index, cot_nodes.reshape(device_count, NODE_DEV, feature_width), cot_edges.reshape(device_count, EDGE_DEV, feature_width))
    (param_sums, spread), (new_nodes, new_edges, edge_grads, local_totals) = lax.scan(one_device, (start_sums, start_spread), device_items)
    grad_nodes = (local_totals.reshape(NODES, feature_width) + spread[:NODES]).astype(jnp.bfloat16)
    return (new_nodes.reshape(NODES, feature_width), new_edges.reshape(EDGES, feature_width), grad_nodes, edge_grads.reshape(EDGES, feature_width), param_sums[0], param_sums[1], param_sums[2], param_sums[3], param_sums[4], param_sums[5], param_sums[6], param_sums[7])
```

```python
import math
from functools import partial

import jax
import jax.numpy as jnp
from jax import lax
from jax.experimental import pallas as pl
from jax.experimental.pallas import tpu as pltpu
from jax.sharding import PartitionSpec as P

EPSILON = 1e-05
LANES = 128
TILE = 1024
STRIP = 512
SMALL = 16
CHUNK = 64
F32 = jnp.float32
BF16 = jnp.bfloat16


def dot(a, b):
    return lax.dot_general(a, b, (((1,), (0,)), ((), ())), preferred_element_type=F32)


def dot_right_t(a, b):
    return lax.dot_general(a, b, (((1,), (1,)), ((), ())), preferred_element_type=F32)


def dot_left_t(a, b):
    return lax.dot_general(a, b, (((0,), (0,)), ((), ())), preferred_element_type=F32)


def strips(rows):
    return [slice(start, start + STRIP) for start in range(0, rows, STRIP)]


def chunks(strip):
    return [slice(start, start + CHUNK) for start in range(strip.start, strip.stop, CHUNK)]


def spread_index(index_row):
    return jnp.transpose(jnp.broadcast_to(index_row, (LANES, index_row.shape[1])))


def lane_hot(column, width):
    lane = lax.broadcasted_iota(jnp.int32, column.shape, 1)
    parts = [
        jnp.where(column == lane + start, 1.0, 0.0).astype(BF16)
        for start in range(0, width, LANES)
    ]
    return jnp.concatenate(parts, axis=1)


def sublane_hot(index_row, width):
    row = lax.broadcasted_iota(jnp.int32, (width, index_row.shape[1]), 0)
    return jnp.where(row == index_row, 1.0, 0.0).astype(BF16)


def sigmoid(values):
    return 0.5 * jnp.tanh(0.5 * values) + 0.5


def normed(values):
    row_mean = jnp.mean(values, axis=-1, keepdims=True)
    centered = values - row_mean
    variance = jnp.mean(centered * centered, axis=-1, keepdims=True)
    inverse = lax.rsqrt(variance + EPSILON)
    return centered * inverse, inverse


def norm_back(cot, gain, hat, inverse):
    product = cot * hat
    scaled = cot * gain
    mean_scaled = jnp.mean(scaled, axis=-1, keepdims=True)
    mean_product = jnp.mean(product * gain, axis=-1, keepdims=True)
    return inverse * (scaled - mean_scaled - hat * mean_product), product


def small_rows(bias_terms, gain_terms, first):
    row = lax.broadcasted_iota(jnp.int32, (SMALL, bias_terms.shape[1]), 0) // 4
    bias, gain = (jnp.sum(terms, axis=0, keepdims=True) for terms in (bias_terms, gain_terms))
    return jnp.where(row == first, bias, jnp.where(row == first + 1, gain, 0.0))


def half_of(number, half):
    return pl.ds(pl.multiple_of(number * half, 16), half)


def halve(total_ref, axis, keep_ref, send_ref):
    place = lax.axis_index(axis)
    half = keep_ref.shape[0] - SMALL
    for target, number in ((keep_ref, place), (send_ref, 1 - place)):
        target[:half, :] = total_ref[half_of(number, half), :]
        target[half:, :] = total_ref[2 * half :, :]


def add(one, other):
    return (one.astype(F32) + other.astype(F32)).astype(BF16)


def block_number(axes, flips):
    number = 0
    for axis in axes:
        own = lax.axis_index(axis)
        number = 2 * number + (1 - own if axis in flips else own)
    return number


def plane_kernel(axes, sides, node_half, keep, got, *targets):
    node_keep, edge_keep = keep.at[:node_half, :], keep.at[node_half:, :]
    node_got, edge_got = got.at[:node_half, :], got.at[node_half:, :]
    edge_rows, node_rows = edge_keep.shape[0] - SMALL, node_keep.shape[0] - SMALL
    edge_part, node_part = edge_rows // len(sides), node_rows // len(sides)
    both = edge_part + node_part
    small = add(
        edge_keep[edge_rows:, :].astype(F32) + edge_got[edge_rows:, :].astype(F32),
        node_keep[node_rows:, :].astype(F32) + node_got[node_rows:, :].astype(F32),
    )
    for flips, target in zip(sides, targets):
        number = block_number(axes, flips)
        rows = half_of(number, edge_part)
        target[:edge_part, :] = add(edge_keep[rows, :], edge_got[rows, :])
        rows = half_of(number, node_part)
        target[edge_part:both, :] = add(node_keep[rows, :], node_got[rows, :])
        end = target.shape[0] - SMALL
        if end > both:
            target[both:end, :] = jnp.zeros((end - both, target.shape[1]), BF16)
        target[end:, :] = small


def line_kernel(sources, *refs):
    parts, targets, total_ref = refs[:sources], refs[sources:-1], refs[-1]
    total = parts[0][...].astype(F32)
    for part in parts[1:]:
        total += part[...].astype(F32)
    total_ref[...] = total.astype(BF16)
    count = len(targets)
    part = targets[0].shape[0] - SMALL
    place = lax.axis_index("z")
    for ahead, target in enumerate(targets):
        target[:part, :] = total_ref[half_of((place + ahead) % count, part), :]
        target[part:, :] = total_ref[count * part :, :]


def total_kernel(*refs):
    parts, (own_ref, small_ref) = refs[:-2], refs[-2:]
    total = parts[0][...].astype(F32)
    for part in parts[1:]:
        total += part[...].astype(F32)
    rows = own_ref.shape[0]
    own_ref[...] = total[:rows, :].astype(BF16)
    small_ref[...] = total[rows:, :]


def join_kernel(*refs):
    parts, (own_ref, top_ref, bottom_ref) = refs[:-3], refs[-3:]
    place = lax.axis_index("z")
    for step, part in enumerate(parts):
        number = lax.bitwise_xor(place, jnp.int32(step))
        own_ref[half_of(number, part.shape[0]), :] = part[...]
    half = top_ref.shape[0]
    top_ref[...] = own_ref[:half, :]
    bottom_ref[...] = own_ref[half:, :]


def finish_kernel(axes, edge_part, node_part, held, *refs):
    pieces, refs = refs[: len(held)], refs[len(held) :]
    wide_ref, sems = refs[-2:]
    if len(refs) == 11:
        small, vectors, refs = refs[0], refs[5:9], refs[1:5] + refs[9:]
        for number, target in enumerate(vectors):
            target[...] = small[4 * number : 4 * number + 4, :][0]
    edge_in, edge_out, node_in, node_out = refs[-6:-2]
    moves, start = [], 0
    for (flips, first), piece in zip(held, pieces):
        last = first + piece.shape[0]
        number = block_number(("core",) + axes, flips)
        for low, size, (one, two) in (
            (0, edge_part, (edge_in, edge_out)),
            (edge_part, node_part, (node_in, node_out)),
        ):
            unit = math.gcd(size, one.shape[0])
            for base in range(low, low + size, unit):
                begin, end = max(first, base), min(last, base + unit)
                if begin >= end:
                    continue
                rows = end - begin
                wide_ref[start : start + rows, :] = piece[begin - first : end - first, :].astype(F32)
                place, split = number * size + base - low, one.shape[0]
                source = wide_ref.at[pl.ds(start, rows), :]
                sem = sems.at[len(moves)]

                def copy(target, row, source=source, sem=sem, rows=rows):
                    into = target.at[pl.ds(pl.multiple_of(row, 8), rows), :]
                    return pltpu.make_async_copy(source, into, sem)

                move = (copy, place < split, one, two, place + begin - base, split)
                moves.append(move)
                run(move, "start")
                start += rows
    for move in moves:
        run(move, "wait")


def run(move, action):
    copy, inside, one, two, row, split = move

    @pl.when(inside)
    def _():
        getattr(copy(one, row), action)()

    @pl.when(jnp.logical_not(inside))
    def _():
        getattr(copy(two, row - split), action)()


def spread_rows(target, slot, rows):
    parts = rows.shape[1] // LANES
    stride = target.shape[0] // rows.shape[0]
    for part in range(parts):
        target[pl.ds(slot * parts + part, rows.shape[0], stride=stride), :] = rows[
            :, part * LANES : (part + 1) * LANES
        ]


def block_rows(source, slot, peers, width):
    parts = width // LANES
    stride = source.shape[0] // peers
    return jnp.concatenate(
        [source[pl.ds(slot * parts + part, peers, stride=stride), :] for part in range(parts)],
        axis=1,
    )


def towards(axes, step):
    return 1 - (lax.axis_index(axes) + step) % 2


def pick_kernel(bands, tiles, halo_ref, far_ref, nodes_ref, far_out_ref, *rims):
    count = nodes_ref.shape[0]
    nodes = nodes_ref[...]
    for number, rim in enumerate(rims):
        axes, first = ((bands, 0), (tiles, 2))[number // 2]
        chosen = halo_ref[0, first : first + 1, :]
        after = halo_ref[0, first + 1 : first + 2, :]
        chosen = jnp.where(towards(axes, number % 2) == 1, after, chosen)
        rim[...] = dot_left_t(sublane_hot(chosen, count), nodes).astype(BF16)
    for slot in range(far_ref.shape[1]):
        hot = sublane_hot(far_ref[0, slot : slot + 1, :], count)
        spread_rows(far_out_ref, slot, dot_left_t(hot, nodes))


def far_place(sender, near, peers, capacity):
    far = sender - near
    return jnp.where(far < 0, sender, near + far % capacity * peers + far // capacity)


def forward_pass(
    step,
    last,
    peers,
    capacity,
    bands,
    tiles,
    count_ref,
    sender_ref,
    receiver_ref,
    edges_ref,
    nodes_ref,
    band_even_ref,
    band_odd_ref,
    tile_even_ref,
    tile_odd_ref,
    far_ref,
    weight_in_ref,
    bias_ref,
    weight_out_ref,
    gain_ref,
    node_weight_in_ref,
    node_bias_ref,
    node_weight_out_ref,
    node_gain_ref,
    cot_nodes_ref,
    edge_out_ref,
    active_ref,
    slope_ref,
    hat_ref,
    inverse_ref,
    table_ref,
    node_out_ref,
    from_gathered_ref,
    from_node_ref,
    keep_ref,
    send_ref,
    projected_ref,
    gathered_ref,
    grads_ref,
    hot_ref,
    wide_ref,
    message_ref,
):
    tile, width = edges_ref.shape
    node_rows = nodes_ref.shape[0]
    slots = table_ref.shape[0]

    @pl.when(step == 0)
    def _():
        table_ref[...] = jnp.zeros_like(table_ref)
        place = 0
        table_ref[:node_rows, :] = nodes_ref[...]
        place += node_rows
        rims = (band_even_ref, band_odd_ref, tile_even_ref, tile_odd_ref)
        for number, rim in enumerate(rims):
            axes = (bands, tiles)[number // 2]
            border = rim.shape[0]
            slot = number // 2 * 2 + towards(axes, number % 2)
            rows = pl.ds(pl.multiple_of(place + slot * border, 32), border)
            table_ref[rows, :] = rim[...]
        place += 4 * border
        for slot in range(capacity):
            table_ref[place : place + peers, :] = block_rows(far_ref, slot, peers, width).astype(
                BF16
            )
            place += peers
        projected_ref[:slots, :] = dot(
            table_ref[...], weight_in_ref[width : 2 * width, :]
        ).astype(BF16)
        projected_ref[slots:, :] = dot(
            nodes_ref[...], weight_in_ref[2 * width :, :]
        ).astype(BF16)
        gathered_ref[...] = jnp.zeros_like(gathered_ref)

    near = node_rows + 4 * band_even_ref.shape[0]
    sender = far_place(sender_ref[...], near, peers, capacity)
    receiver = receiver_ref[...]
    halves = strips(tile)

    def gather(strip):
        senders = spread_index(sender[:, strip])
        receivers = spread_index(receiver[:, strip])
        for rows in chunks(strip):
            here = slice(rows.start - strip.start, rows.stop - strip.start)
            hot_ref[rows, :slots] = lane_hot(senders[here, :], slots)
            hot_ref[rows, slots:] = lane_hot(receivers[here, :], node_rows)
        wide_ref[strip, :] = dot(edges_ref[strip, :], weight_in_ref[:width, :]) + dot(
            hot_ref[strip, :], projected_ref[...]
        )

    def activate(strip):
        for rows in chunks(strip):
            first = wide_ref[rows, :] + bias_ref[...]
            gate = sigmoid(first)
            active = first * gate
            message_ref[rows, :] = active.astype(BF16)
            active_ref[rows, :] = active.astype(BF16)
            slope_ref[rows, :] = (gate + active * (1.0 - gate)).astype(BF16)
        wide_ref[strip, :] = dot(message_ref[strip, :], weight_out_ref[...])

    def send(strip):
        for rows in chunks(strip):
            hat, inverse = normed(wide_ref[rows, :])
            hat_ref[rows, :] = hat.astype(BF16)
            inverse_ref[rows, :] = jnp.broadcast_to(inverse, (CHUNK, inverse_ref.shape[1]))
            place = lax.broadcasted_iota(jnp.int32, (CHUNK, 1), 0) + (step * tile + rows.start)
            message = jnp.where(place < count_ref[0], hat * gain_ref[...], 0.0)
            message_ref[rows, :] = message.astype(BF16)
            edge_out_ref[rows, :] = (edges_ref[rows, :].astype(F32) + message).astype(BF16)

    for work in (gather, activate, send):
        for strip in halves:
            work(strip)
    gathered_ref[...] += dot(sublane_hot(receiver, node_rows), message_ref[...])

    @pl.when(step == last)
    def _():
        nodes = nodes_ref[...]
        gathered = gathered_ref[...].astype(BF16)
        first = (
            dot(nodes, node_weight_in_ref[:width, :])
            + dot(gathered, node_weight_in_ref[width:, :])
            + node_bias_ref[...]
        )
        gate = sigmoid(first)
        active_wide = first * gate
        slope = gate + active_wide * (1.0 - gate)
        active = active_wide.astype(BF16)
        hat, inverse = normed(dot(active, node_weight_out_ref[...]))
        gain = node_gain_ref[...]
        node_out_ref[...] = (nodes.astype(F32) + hat * gain).astype(BF16)
        cot = cot_nodes_ref[...].astype(F32)
        back, product = norm_back(cot, gain, hat, inverse)
        second_back = back.astype(BF16)
        first_wide = dot_right_t(second_back, node_weight_out_ref[...]) * slope
        first_back = first_wide.astype(BF16)
        from_node_ref[...] = cot + dot_right_t(first_back, node_weight_in_ref[:width, :])
        from_gathered_ref[...] = dot_right_t(
            first_back, node_weight_in_ref[width:, :]
        ).astype(BF16)
        grads_ref[:width, :] = dot_left_t(nodes, first_back).astype(BF16)
        grads_ref[width : 2 * width, :] = dot_left_t(gathered, first_back).astype(BF16)
        grads_ref[2 * width : 3 * width, :] = dot_left_t(active, second_back).astype(BF16)
        grads_ref[3 * width :, :] = small_rows(first_wide, product, 2).astype(BF16)
        halve(grads_ref, "core", keep_ref, send_ref)


def backward_pass(
    step,
    last,
    peers,
    capacity,
    near,
    bands,
    tiles,
    count_ref,
    sender_ref,
    receiver_ref,
    edges_ref,
    cot_ref,
    active_ref,
    slope_ref,
    hat_ref,
    inverse_ref,
    table_ref,
    from_gathered_ref,
    from_node_ref,
    weight_in_ref,
    weight_out_ref,
    gain_ref,
    edge_grad_ref,
    totals_ref,
    back_far_ref,
    band_even_ref,
    band_odd_ref,
    tile_even_ref,
    tile_odd_ref,
    keep_ref,
    send_ref,
    sums_ref,
    in_sum_ref,
    out_sum_ref,
    gain_sum_ref,
    grads_ref,
    wide_ref,
    second_ref,
    first_ref,
):
    tile, width = edges_ref.shape
    node_rows = from_gathered_ref.shape[0]
    slots = table_ref.shape[0]

    @pl.when(step == 0)
    def _():
        sums_ref[...] = jnp.zeros_like(sums_ref)
        in_sum_ref[...] = jnp.zeros_like(in_sum_ref)
        out_sum_ref[...] = jnp.zeros_like(out_sum_ref)
        gain_sum_ref[...] = jnp.zeros_like(gain_sum_ref)

    sender = far_place(sender_ref[...], near, peers, capacity)
    receiver = receiver_ref[...]
    halves = strips(tile)
    for strip in halves:
        hot = lane_hot(spread_index(receiver[:, strip]), node_rows)
        wide_ref[strip, :] = dot(hot, from_gathered_ref[...])

    def normalize(strip):
        gain_sum = gain_sum_ref[...]
        for rows in chunks(strip):
            place = lax.broadcasted_iota(jnp.int32, (CHUNK, 1), 0) + (step * tile + rows.start)
            cot = cot_ref[rows, :].astype(F32) + wide_ref[rows, :]
            cot = jnp.where(place < count_ref[0], cot, 0.0)
            hat = hat_ref[rows, :].astype(F32)
            back, product = norm_back(cot, gain_ref[...], hat, inverse_ref[rows, 0:1])
            gain_sum += jnp.sum(product.reshape(CHUNK // 8, 8, width), axis=0)
            second_ref[rows, :] = back.astype(BF16)
        gain_sum_ref[...] = gain_sum
        wide_ref[strip, :] = dot_right_t(second_ref[strip, :], weight_out_ref[...])

    def activate(strip):
        for rows in chunks(strip):
            first_ref[rows, :] = (wide_ref[rows, :] * slope_ref[rows, :].astype(F32)).astype(BF16)
        wide_ref[strip, :] = dot_right_t(first_ref[strip, :], weight_in_ref[:width, :])

    for work in (normalize, activate):
        for strip in halves:
            work(strip)
    out_sum_ref[...] += dot_left_t(active_ref[...], second_ref[...])
    for rows in chunks(slice(0, tile)):
        edge_grad_ref[rows, :] = (cot_ref[rows, :].astype(F32) + wide_ref[rows, :]).astype(BF16)
    first_back = first_ref[...]
    in_sum_ref[...] += dot_left_t(edges_ref[...], first_back)
    sums_ref[:slots, :] += dot(sublane_hot(sender, slots), first_back)
    sums_ref[slots:, :] += dot(sublane_hot(receiver, node_rows), first_back)

    @pl.when(step == last)
    def _():
        sent = sums_ref[:slots, :].astype(BF16)
        received_wide = sums_ref[slots:, :]
        received = received_wide.astype(BF16)
        grads_ref[:width, :] = in_sum_ref[...].astype(BF16)
        grads_ref[width : 2 * width, :] = dot_left_t(table_ref[...], sent).astype(BF16)
        grads_ref[2 * width : 3 * width, :] = dot_left_t(
            table_ref[:node_rows, :], received
        ).astype(BF16)
        grads_ref[3 * width : 4 * width, :] = out_sum_ref[...].astype(BF16)
        grads_ref[4 * width :, :] = small_rows(received_wide, gain_sum_ref[...], 0).astype(BF16)
        halve(grads_ref, "core", keep_ref, send_ref)
        sent_back = dot_right_t(sent, weight_in_ref[width : 2 * width, :])
        totals_ref[...] = (
            from_node_ref[...]
            + dot_right_t(received, weight_in_ref[2 * width :, :])
            + sent_back[:node_rows, :]
        )
        place = node_rows
        rims = (band_even_ref, band_odd_ref, tile_even_ref, tile_odd_ref)
        for number, rim in enumerate(rims):
            axes, first = ((bands, place), (tiles, place + 2 * rim.shape[0]))[number // 2]
            before = sent_back[first : first + rim.shape[0], :]
            after = sent_back[first + rim.shape[0] : first + 2 * rim.shape[0], :]
            rim[...] = jnp.where(towards(axes, number % 2) == 1, after, before).astype(BF16)
        place += 4 * rims[0].shape[0]
        for slot in range(capacity):
            spread_rows(back_far_ref, slot, sent_back[place : place + peers, :])
            place += peers


def passes_kernel(peers, capacity, near, bands, tiles, *refs):
    ins, outs, scratch = refs[:20], refs[20:31], refs[31:]
    count, sender, receiver, edges, cot = ins[:5]
    nodes, *halo, weight_in, bias, weight_out, gain = ins[5:15]
    edge_out, edge_grad, node_out, totals, back_far, *back_rims, keep, send = outs
    active, slope, hat, inverse, table, from_gathered, from_node = scratch[:7]
    projected, gathered, grads, hot, wide, second, first, sums, in_sum, out_sum, gain_sum = scratch[7:]
    tile, width = edges.shape
    steps = pl.num_programs(0) // 2
    step = lax.rem(pl.program_id(0), steps)
    rows = pl.ds(pl.multiple_of(step * tile, tile), tile)
    saved = [ref.at[rows, :] for ref in (active, slope, hat, inverse)]
    node_half = 3 * width // 2 + SMALL
    node_ends = [ref.at[:node_half, :] for ref in (keep, send)]
    edge_ends = [ref.at[node_half:, :] for ref in (keep, send)]

    @pl.when(pl.program_id(0) < steps)
    def _():
        forward_pass(
            step,
            steps - 1,
            peers,
            capacity,
            bands,
            tiles,
            count,
            sender,
            receiver,
            edges,
            nodes,
            *halo,
            weight_in,
            bias,
            weight_out,
            gain,
            *ins[15:],
            edge_out,
            *saved,
            table,
            node_out,
            from_gathered,
            from_node,
            *node_ends,
            projected,
            gathered,
            grads.at[: 3 * width + SMALL, :],
            hot,
            wide,
            second,
        )

    @pl.when(pl.program_id(0) >= steps)
    def _():
        backward_pass(
            step,
            steps - 1,
            peers,
            capacity,
            near,
            bands,
            tiles,
            count,
            sender,
            receiver,
            edges,
            cot,
            *saved,
            table,
            from_gathered,
            from_node,
            weight_in,
            weight_out,
            gain,
            edge_grad,
            totals,
            back_far,
            *back_rims,
            *edge_ends,
            sums,
            in_sum,
            out_sum,
            gain_sum,
            grads,
            wide,
            second,
            first,
        )


def return_kernel(bands, tiles, halo_ref, far_ref, totals_ref, returned_ref, *refs):
    rims, out_ref = refs[:-1], refs[-1]
    count, width = totals_ref.shape
    capacity, peers = far_ref.shape[1:]
    total = totals_ref[...]
    for number, rim in enumerate(rims):
        axes, first = ((bands, 0), (tiles, 2))[number // 2]
        chosen = halo_ref[0, first : first + 1, :]
        after = halo_ref[0, first + 1 : first + 2, :]
        chosen = jnp.where(towards(axes, number % 2) == 1, after, chosen)
        total += dot(sublane_hot(chosen, count), rim[...])
    for slot in range(capacity):
        hot = sublane_hot(far_ref[0, slot : slot + 1, :], count)
        total += dot(hot, block_rows(returned_ref, slot, peers, width).astype(BF16))
    out_ref[...] = total.astype(BF16)


def swap(array, axes, step, wrap):
    size = lax.axis_size(axes)
    pairs = []
    for low in range(step, size if wrap else size - 1, 2):
        high = (low + 1) % size
        pairs += [(low, high), (high, low)]
    return lax.ppermute(array, axes, pairs)


def after(arrays, *others):
    return lax.optimization_barrier((arrays, others))[0]


def limits(megabytes=62):
    return pltpu.CompilerParams(
        dimension_semantics=("arbitrary",), vmem_limit_bytes=megabytes * 2**20
    )


def shards(
    x_axes,
    y_axes,
    node_latents,
    edge_latents,
    edge_count,
    receiver,
    sender,
    halo_send,
    far_send,
    edge_weight_in,
    edge_bias,
    edge_weight_out,
    edge_gain,
    node_weight_in,
    node_bias,
    node_weight_out,
    node_gain,
    cot_nodes,
    cot_edges,
):
    node_rows, width = node_latents.shape
    edge_rows = edge_latents.shape[0]
    border = halo_send.shape[2]
    peers = far_send.shape[1]
    capacity = far_send.shape[2]
    rims = 4 * border
    fars = peers * capacity
    used = node_rows + rims + fars
    slots = -(-used // LANES) * LANES
    tile = TILE
    steps = edge_rows // tile

    far_send = jnp.swapaxes(far_send, 1, 2)
    sender = sender.reshape(1, edge_rows)
    receiver = receiver.reshape(1, edge_rows)
    bands = (*x_axes, "core")
    tiles = ("z", *y_axes)
    everyone = bands + tiles

    def exchanged(blocks):
        parts = blocks.reshape(peers, -1, LANES)
        return lax.all_to_all(parts, everyone, split_axis=0, concat_axis=0, tiled=True).reshape(
            -1, LANES
        )

    def call(kernel, name, out_shape, *args, scratch=()):
        return pl.pallas_call(
            kernel,
            out_shape=out_shape,
            scratch_shapes=scratch,
            compiler_params=pltpu.CompilerParams(vmem_limit_bytes=62 * 2**20),
            name=name,
        )(*args)

    def packed(*shape):
        return jax.ShapeDtypeStruct(shape, BF16)

    def wide(*shape):
        return jax.ShapeDtypeStruct(shape, F32)

    def across(array, axes):
        last = 2 ** len(axes) - 1
        return lax.ppermute(array, axes, [(i, last - i) for i in range(last + 1)])

    def ahead(array, step):
        size = lax.axis_size("z")
        return lax.ppermute(array, "z", [(i, (i + step) % size) for i in range(size)])

    rim_shape = jax.ShapeDtypeStruct((border, width), BF16)
    far_shape = jax.ShapeDtypeStruct((fars * width // LANES, LANES), F32)
    far_rows, *rim_rows = call(
        partial(pick_kernel, bands, tiles),
        "pick",
        (far_shape,) + (rim_shape,) * 4,
        halo_send,
        far_send,
        node_latents,
    )
    def swapped(rims):
        return [
            swap(rims[0], bands, 0, False),
            swap(rims[1], bands, 1, False),
            swap(rims[2], tiles, 0, True),
            swap(rims[3], tiles, 1, True),
        ]

    got_rims = swapped(rim_rows)
    incoming = exchanged(far_rows)

    def whole(*shape):
        return pl.BlockSpec(shape, lambda i: (0,) * len(shape))

    both = pl.BlockSpec((tile, width), lambda i: (i % steps, 0))
    ahead_only = pl.BlockSpec((tile, width), lambda i: (jnp.minimum(i, steps - 1), 0))
    back_only = pl.BlockSpec((tile, width), lambda i: (jnp.maximum(i - steps, 0), 0))
    index_spec = pl.BlockSpec((1, tile), lambda i: (0, i % steps))
    scalar = pl.BlockSpec(memory_space=pltpu.SMEM)
    rim_spec = whole(border, width)
    far_spec = whole(*far_shape.shape)
    line, node_spec, square = whole(1, width), whole(node_rows, width), whole(width, width)
    node_half = 3 * width // 2 + SMALL
    edge_half = 4 * width // 2 + SMALL
    flat = packed(edge_rows, width)
    core_half = packed(node_half + edge_half, width)
    (edge_out, edge_grad, node_out, totals, back_far, *back_rims, keep, send) = pl.pallas_call(
        partial(passes_kernel, peers, capacity, node_rows + rims, bands, tiles),
        grid=(2 * steps,),
        in_specs=[scalar, index_spec, index_spec, both, back_only, node_spec]
        + [rim_spec] * 4
        + [far_spec, whole(3 * width, width), line, square, line]
        + [whole(2 * width, width), line, square, line, node_spec],
        out_specs=(ahead_only, back_only, node_spec, node_spec, far_spec)
        + (rim_spec,) * 4
        + (whole(*core_half.shape),) * 2,
        out_shape=(flat, flat, packed(node_rows, width), wide(node_rows, width), far_shape)
        + (rim_shape,) * 4
        + (core_half,) * 2,
        scratch_shapes=[
            pltpu.VMEM((edge_rows, width), BF16),
            pltpu.VMEM((edge_rows, width), BF16),
            pltpu.VMEM((edge_rows, width), BF16),
            pltpu.VMEM((edge_rows, LANES), F32),
            pltpu.VMEM((slots, width), BF16),
            pltpu.VMEM((node_rows, width), BF16),
            pltpu.VMEM((node_rows, width), F32),
            pltpu.VMEM((slots + node_rows, width), BF16),
            pltpu.VMEM((node_rows, width), F32),
            pltpu.VMEM((4 * width + SMALL, width), BF16),
            pltpu.VMEM((tile, slots + node_rows), BF16),
            pltpu.VMEM((tile, width), F32),
            pltpu.VMEM((tile, width), BF16),
            pltpu.VMEM((tile, width), BF16),
            pltpu.VMEM((slots + node_rows, width), F32),
            pltpu.VMEM((width, width), F32),
            pltpu.VMEM((width, width), F32),
            pltpu.VMEM((8, width), F32),
        ],
        compiler_params=limits(),
        cost_estimate=pl.CostEstimate(
            flops=2 * 10**10, bytes_accessed=2 * 10**7, transcendentals=10**6
        ),
        name="passes",
    )(
        edge_count,
        sender,
        receiver,
        edge_latents,
        cot_edges,
        node_latents,
        *got_rims,
        incoming,
        edge_weight_in,
        edge_bias.reshape(1, width),
        edge_weight_out,
        edge_gain.reshape(1, width),
        node_weight_in,
        node_bias.reshape(1, width),
        node_weight_out,
        node_gain.reshape(1, width),
        cot_nodes,
    )
    core_got = across(send, ("core",))
    plane = x_axes + y_axes
    sides = [()]
    for axis in plane:
        sides += [flips + (axis,) for flips in sides]
    depth = lax.axis_size("z")
    edge_part = (edge_half - SMALL) // len(sides)
    node_part = (node_half - SMALL) // len(sides)
    part = -(-(edge_part + node_part) // (16 * depth)) * 16
    parts = call(
        partial(plane_kernel, plane, sides, node_half),
        "plane",
        (packed(part * depth + SMALL, width),) * len(sides),
        keep,
        core_got,
    )
    got = [across(array, flips) for array, flips in zip(parts[1:], sides[1:])]

    back_far, back_rims = after((back_far, back_rims), parts)
    returned_rims = swapped(back_rims)
    returned = exchanged(back_far)
    parts = call(
        partial(line_kernel, len(sides)),
        "line",
        (packed(part + SMALL, width),) * depth,
        *after((parts[0], *got), returned, returned_rims),
        scratch=[pltpu.VMEM((part * depth + SMALL, width), BF16)],
    )
    got = [ahead(parts[step], step) for step in range(1, depth)]
    own, small = call(
        total_kernel, "total", (packed(part, width), wide(SMALL, width)), parts[0], *got
    )
    lines, bit = {0: own}, depth // 2
    while bit:
        for step, piece in list(lines.items()):
            lines[step + bit] = lax.ppermute(piece, "z", [(i, i ^ bit) for i in range(depth)])
        bit //= 2
    middle = part * depth // 2
    own, top, bottom = call(
        join_kernel,
        "join",
        (packed(2 * middle, width), packed(middle, width), packed(middle, width)),
        *(lines[step] for step in range(depth)),
    )
    grad_nodes = call(
        partial(return_kernel, bands, tiles),
        "returned",
        packed(node_rows, width),
        *after((halo_send, far_send, totals, returned, *returned_rims), own),
    )

    copies = edge_part // math.gcd(edge_part, 3 * width) + node_part // math.gcd(node_part, 2 * width)
    anywhere, here = pl.BlockSpec(memory_space=pl.ANY), pl.BlockSpec(memory_space=pltpu.VMEM)
    whole_grads = (wide(3 * width, width), wide(width, width))
    whole_grads += (wide(2 * width, width), wide(width, width))

    def finished(pieces, extra):
        rows = sum(piece.shape[0] for piece in pieces.values())
        first = len(extra) == 1
        return pl.pallas_call(
            partial(finish_kernel, plane, edge_part, node_part, tuple(pieces.keys())),
            out_shape=whole_grads + (wide(width),) * (4 if first else 0),
            in_specs=[here] * len(pieces) + ([here] if first else [anywhere] * 4),
            out_specs=(anywhere,) * 4 + (here,) * (4 if first else 0),
            input_output_aliases={} if first else {len(pieces) + i: i for i in range(4)},
            scratch_shapes=[
                pltpu.VMEM((rows, width), F32),
                pltpu.SemaphoreType.DMA((copies * len(pieces),)),
            ],
            compiler_params=pltpu.CompilerParams(vmem_limit_bytes=62 * 2**20),
            name="finish",
        )(*pieces.values(), *extra)

    held = {((), 0): own}
    if len(plane) == 2:
        one, two = plane
        held[(one,), middle] = across(bottom, (one,))
        held[(two,), 0] = across(top, (two,))
        held[(one,), 0] = across(top, (one,))
        held[(two,), middle] = across(bottom, (two,))
        late = {
            (plane, 0): across(held[(two,), 0], (one,)),
            (plane, middle): across(held[(one,), middle], (two,)),
        }
        for flips in ((one,), (two,)):
            for first in (0, middle):
                late[flips + ("core",), first] = across(held[flips, first], ("core",))
        held[("core",), 0] = across(own, ("core",))
        *grads, bias, gain, node_small, node_scale = finished(held, (after(small, grad_nodes),))
        for first in (0, middle):
            piece = after(late[plane, first], bias)
            late[plane + ("core",), first] = across(piece, ("core",))
    else:
        for flips in sides[1:]:
            held[flips, 0] = across(own, flips)
        late = {
            (flips + ("core",), first): across(piece, ("core",))
            for (flips, first), piece in held.items()
        }
        *grads, bias, gain, node_small, node_scale = finished(held, (small,))
    grads = finished(late, grads)
    return (
        node_out,
        edge_out,
        grad_nodes,
        edge_grad,
        grads[0],
        bias,
        grads[1],
        gain,
        grads[2],
        node_small,
        grads[3],
        node_scale,
    )


def solution(mesh):
    bands, tiles = mesh.devices.shape
    x_axes = tuple(f"x{bit}" for bit in range((bands // 2).bit_length() - 1))
    y_axes = tuple(f"y{bit}" for bit in range((tiles.bit_length() - 1) // 2))
    names = (*x_axes, "core", "z", *y_axes)
    shape = (2,) * len(x_axes) + (2, tiles // 2 ** len(y_axes)) + (2,) * len(y_axes)
    cores = jax.sharding.Mesh(mesh.devices.reshape(shape), names)
    spread = P(names, None)
    line = P(names)
    cube = P(names, None, None)
    return jax.shard_map(
        partial(shards, x_axes, y_axes),
        mesh=cores,
        in_specs=(spread, spread, line, line, line, cube, cube) + (P(),) * 8 + (spread, spread),
        out_specs=(spread, spread, spread, spread) + (P(),) * 8,
        check_vma=False,
    )
```

```python
import math
from functools import partial

import jax
import jax.numpy as jnp
from jax import lax
from jax.experimental import pallas as pl
from jax.experimental.pallas import tpu as pltpu
from jax.sharding import PartitionSpec as P

EPSILON = 1e-05
LANES = 128
TILE = 1024
STRIP = 512
SMALL = 16
CHUNK = 64
F32 = jnp.float32
BF16 = jnp.bfloat16


def dot(a, b):
    return lax.dot_general(a, b, (((1,), (0,)), ((), ())), preferred_element_type=F32)


def dot_right_t(a, b):
    return lax.dot_general(a, b, (((1,), (1,)), ((), ())), preferred_element_type=F32)


def dot_left_t(a, b):
    return lax.dot_general(a, b, (((0,), (0,)), ((), ())), preferred_element_type=F32)


def strips(rows):
    return [slice(start, start + STRIP) for start in range(0, rows, STRIP)]


def chunks(strip):
    return [slice(start, start + CHUNK) for start in range(strip.start, strip.stop, CHUNK)]


def spread_index(index_row):
    return jnp.transpose(jnp.broadcast_to(index_row, (LANES, index_row.shape[1])))


def lane_hot(column, width):
    lane = lax.broadcasted_iota(jnp.int32, column.shape, 1)
    parts = [
        jnp.where(column == lane + start, 1.0, 0.0).astype(BF16)
        for start in range(0, width, LANES)
    ]
    return jnp.concatenate(parts, axis=1)


def sublane_hot(index_row, width):
    row = lax.broadcasted_iota(jnp.int32, (width, index_row.shape[1]), 0)
    return jnp.where(row == index_row, 1.0, 0.0).astype(BF16)


def sigmoid(values):
    return 0.5 * jnp.tanh(0.5 * values) + 0.5


def normed(values):
    row_mean = jnp.mean(values, axis=-1, keepdims=True)
    centered = values - row_mean
    variance = jnp.mean(centered * centered, axis=-1, keepdims=True)
    inverse = lax.rsqrt(variance + EPSILON)
    return centered * inverse, inverse


def norm_back(cot, gain, hat, inverse):
    product = cot * hat
    scaled = cot * gain
    mean_scaled = jnp.mean(scaled, axis=-1, keepdims=True)
    mean_product = jnp.mean(product * gain, axis=-1, keepdims=True)
    return inverse * (scaled - mean_scaled - hat * mean_product), product


def small_rows(bias_terms, gain_terms, first):
    row = lax.broadcasted_iota(jnp.int32, (SMALL, bias_terms.shape[1]), 0) // 4
    bias, gain = (jnp.sum(terms, axis=0, keepdims=True) for terms in (bias_terms, gain_terms))
    return jnp.where(row == first, bias, jnp.where(row == first + 1, gain, 0.0))


def half_of(number, half):
    return pl.ds(pl.multiple_of(number * half, 16), half)


def halve(total_ref, axis, keep_ref, send_ref):
    place = lax.axis_index(axis)
    half = keep_ref.shape[0] - SMALL
    for target, number in ((keep_ref, place), (send_ref, 1 - place)):
        target[:half, :] = total_ref[half_of(number, half), :]
        target[half:, :] = total_ref[2 * half :, :]


def add(one, other):
    return (one.astype(F32) + other.astype(F32)).astype(BF16)


def block_number(axes, flips):
    number = 0
    for axis in axes:
        own = lax.axis_index(axis)
        number = 2 * number + (1 - own if axis in flips else own)
    return number


def plane_kernel(axes, sides, node_half, keep, got, *targets):
    node_keep, edge_keep = keep.at[:node_half, :], keep.at[node_half:, :]
    node_got, edge_got = got.at[:node_half, :], got.at[node_half:, :]
    edge_rows, node_rows = edge_keep.shape[0] - SMALL, node_keep.shape[0] - SMALL
    edge_part, node_part = edge_rows // len(sides), node_rows // len(sides)
    both = edge_part + node_part
    small = add(
        edge_keep[edge_rows:, :].astype(F32) + edge_got[edge_rows:, :].astype(F32),
        node_keep[node_rows:, :].astype(F32) + node_got[node_rows:, :].astype(F32),
    )
    for flips, target in zip(sides, targets):
        number = block_number(axes, flips)
        rows = half_of(number, edge_part)
        target[:edge_part, :] = add(edge_keep[rows, :], edge_got[rows, :])
        rows = half_of(number, node_part)
        target[edge_part:both, :] = add(node_keep[rows, :], node_got[rows, :])
        end = target.shape[0] - SMALL
        if end > both:
            target[both:end, :] = jnp.zeros((end - both, target.shape[1]), BF16)
        target[end:, :] = small


def line_kernel(sources, *refs):
    parts, targets, total_ref = refs[:sources], refs[sources:-1], refs[-1]
    total = parts[0][...].astype(F32)
    for part in parts[1:]:
        total += part[...].astype(F32)
    total_ref[...] = total.astype(BF16)
    count = len(targets)
    part = targets[0].shape[0] - SMALL
    place = lax.axis_index("z")
    for ahead, target in enumerate(targets):
        target[:part, :] = total_ref[half_of((place + ahead) % count, part), :]
        target[part:, :] = total_ref[count * part :, :]


def total_kernel(*refs):
    parts, (own_ref, small_ref) = refs[:-2], refs[-2:]
    total = parts[0][...].astype(F32)
    for part in parts[1:]:
        total += part[...].astype(F32)
    rows = own_ref.shape[0]
    own_ref[...] = total[:rows, :].astype(BF16)
    small_ref[...] = total[rows:, :]


def join_kernel(*refs):
    parts, (own_ref, top_ref, bottom_ref) = refs[:-3], refs[-3:]
    place = lax.axis_index("z")
    for step, part in enumerate(parts):
        number = lax.bitwise_xor(place, jnp.int32(step))
        own_ref[half_of(number, part.shape[0]), :] = part[...]
    half = top_ref.shape[0]
    top_ref[...] = own_ref[:half, :]
    bottom_ref[...] = own_ref[half:, :]


def finish_kernel(axes, edge_part, node_part, held, *refs):
    pieces, refs = refs[: len(held)], refs[len(held) :]
    wide_ref, sems = refs[-2:]
    if len(refs) == 11:
        small, vectors, refs = refs[0], refs[5:9], refs[1:5] + refs[9:]
        for number, target in enumerate(vectors):
            target[...] = small[4 * number : 4 * number + 4, :][0]
    edge_in, edge_out, node_in, node_out = refs[-6:-2]
    moves, start = [], 0
    for (flips, first), piece in zip(held, pieces):
        last = first + piece.shape[0]
        number = block_number(("core",) + axes, flips)
        for low, size, (one, two) in (
            (0, edge_part, (edge_in, edge_out)),
            (edge_part, node_part, (node_in, node_out)),
        ):
            unit = math.gcd(size, one.shape[0])
            for base in range(low, low + size, unit):
                begin, end = max(first, base), min(last, base + unit)
                if begin >= end:
                    continue
                rows = end - begin
                wide_ref[start : start + rows, :] = piece[begin - first : end - first, :].astype(F32)
                place, split = number * size + base - low, one.shape[0]
                source = wide_ref.at[pl.ds(start, rows), :]
                sem = sems.at[len(moves)]

                def copy(target, row, source=source, sem=sem, rows=rows):
                    into = target.at[pl.ds(pl.multiple_of(row, 8), rows), :]
                    return pltpu.make_async_copy(source, into, sem)

                move = (copy, place < split, one, two, place + begin - base, split)
                moves.append(move)
                run(move, "start")
                start += rows
    for move in moves:
        run(move, "wait")


def run(move, action):
    copy, inside, one, two, row, split = move

    @pl.when(inside)
    def _():
        getattr(copy(one, row), action)()

    @pl.when(jnp.logical_not(inside))
    def _():
        getattr(copy(two, row - split), action)()


def spread_rows(target, slot, rows):
    parts = rows.shape[1] // LANES
    stride = target.shape[0] // rows.shape[0]
    for part in range(parts):
        target[pl.ds(slot * parts + part, rows.shape[0], stride=stride), :] = rows[
            :, part * LANES : (part + 1) * LANES
        ]


def block_rows(source, slot, peers, width):
    parts = width // LANES
    stride = source.shape[0] // peers
    return jnp.concatenate(
        [source[pl.ds(slot * parts + part, peers, stride=stride), :] for part in range(parts)],
        axis=1,
    )


def towards(axes, step):
    return 1 - (lax.axis_index(axes) + step) % 2


def pick_kernel(bands, tiles, halo_ref, far_ref, nodes_ref, far_out_ref, *rims):
    count = nodes_ref.shape[0]
    nodes = nodes_ref[...]
    for number, rim in enumerate(rims):
        axes, first = ((bands, 0), (tiles, 2))[number // 2]
        chosen = halo_ref[0, first : first + 1, :]
        after = halo_ref[0, first + 1 : first + 2, :]
        chosen = jnp.where(towards(axes, number % 2) == 1, after, chosen)
        rim[...] = dot_left_t(sublane_hot(chosen, count), nodes).astype(BF16)
    for slot in range(far_ref.shape[1]):
        hot = sublane_hot(far_ref[0, slot : slot + 1, :], count)
        spread_rows(far_out_ref, slot, dot_left_t(hot, nodes))


def far_place(sender, near, peers, capacity):
    far = sender - near
    return jnp.where(far < 0, sender, near + far % capacity * peers + far // capacity)


def forward_pass(
    step,
    last,
    peers,
    capacity,
    bands,
    tiles,
    count_ref,
    sender_ref,
    receiver_ref,
    edges_ref,
    nodes_ref,
    band_even_ref,
    band_odd_ref,
    tile_even_ref,
    tile_odd_ref,
    far_ref,
    weight_in_ref,
    bias_ref,
    weight_out_ref,
    gain_ref,
    node_weight_in_ref,
    node_bias_ref,
    node_weight_out_ref,
    node_gain_ref,
    cot_nodes_ref,
    edge_out_ref,
    active_ref,
    slope_ref,
    hat_ref,
    inverse_ref,
    table_ref,
    node_out_ref,
    from_gathered_ref,
    from_node_ref,
    keep_ref,
    send_ref,
    projected_ref,
    gathered_ref,
    grads_ref,
    hot_ref,
    wide_ref,
    message_ref,
):
    tile, width = edges_ref.shape
    node_rows = nodes_ref.shape[0]
    slots = table_ref.shape[0]

    @pl.when(step == 0)
    def _():
        table_ref[...] = jnp.zeros_like(table_ref)
        place = 0
        table_ref[:node_rows, :] = nodes_ref[...]
        place += node_rows
        rims = (band_even_ref, band_odd_ref, tile_even_ref, tile_odd_ref)
        for number, rim in enumerate(rims):
            axes = (bands, tiles)[number // 2]
            border = rim.shape[0]
            slot = number // 2 * 2 + towards(axes, number % 2)
            rows = pl.ds(pl.multiple_of(place + slot * border, 32), border)
            table_ref[rows, :] = rim[...]
        place += 4 * border
        for slot in range(capacity):
            table_ref[place : place + peers, :] = block_rows(far_ref, slot, peers, width).astype(
                BF16
            )
            place += peers
        projected_ref[:slots, :] = dot(
            table_ref[...], weight_in_ref[width : 2 * width, :]
        ).astype(BF16)
        projected_ref[slots:, :] = dot(
            nodes_ref[...], weight_in_ref[2 * width :, :]
        ).astype(BF16)
        gathered_ref[...] = jnp.zeros_like(gathered_ref)

    near = node_rows + 4 * band_even_ref.shape[0]
    sender = far_place(sender_ref[...], near, peers, capacity)
    receiver = receiver_ref[...]
    halves = strips(tile)

    def gather(strip):
        senders = spread_index(sender[:, strip])
        receivers = spread_index(receiver[:, strip])
        for rows in chunks(strip):
            here = slice(rows.start - strip.start, rows.stop - strip.start)
            hot_ref[rows, :slots] = lane_hot(senders[here, :], slots)
            hot_ref[rows, slots:] = lane_hot(receivers[here, :], node_rows)
        wide_ref[strip, :] = dot(edges_ref[strip, :], weight_in_ref[:width, :]) + dot(
            hot_ref[strip, :], projected_ref[...]
        )

    def activate(strip):
        for rows in chunks(strip):
            first = wide_ref[rows, :] + bias_ref[...]
            gate = sigmoid(first)
            active = first * gate
            message_ref[rows, :] = active.astype(BF16)
            active_ref[rows, :] = active.astype(BF16)
            slope_ref[rows, :] = (gate + active * (1.0 - gate)).astype(BF16)
        wide_ref[strip, :] = dot(message_ref[strip, :], weight_out_ref[...])

    def send(strip):
        for rows in chunks(strip):
            hat, inverse = normed(wide_ref[rows, :])
            hat_ref[rows, :] = hat.astype(BF16)
            inverse_ref[rows, :] = jnp.broadcast_to(inverse, (CHUNK, inverse_ref.shape[1]))
            place = lax.broadcasted_iota(jnp.int32, (CHUNK, 1), 0) + (step * tile + rows.start)
            message = jnp.where(place < count_ref[0], hat * gain_ref[...], 0.0)
            message_ref[rows, :] = message.astype(BF16)
            edge_out_ref[rows, :] = (edges_ref[rows, :].astype(F32) + message).astype(BF16)

    for work in (gather, activate, send):
        for strip in halves:
            work(strip)
    gathered_ref[...] += dot(sublane_hot(receiver, node_rows), message_ref[...])

    @pl.when(step == last)
    def _():
        nodes = nodes_ref[...]
        gathered = gathered_ref[...].astype(BF16)
        first = (
            dot(nodes, node_weight_in_ref[:width, :])
            + dot(gathered, node_weight_in_ref[width:, :])
            + node_bias_ref[...]
        )
        gate = sigmoid(first)
        active_wide = first * gate
        slope = gate + active_wide * (1.0 - gate)
        active = active_wide.astype(BF16)
        hat, inverse = normed(dot(active, node_weight_out_ref[...]))
        gain = node_gain_ref[...]
        node_out_ref[...] = (nodes.astype(F32) + hat * gain).astype(BF16)
        cot = cot_nodes_ref[...].astype(F32)
        back, product = norm_back(cot, gain, hat, inverse)
        second_back = back.astype(BF16)
        first_wide = dot_right_t(second_back, node_weight_out_ref[...]) * slope
        first_back = first_wide.astype(BF16)
        from_node_ref[...] = cot + dot_right_t(first_back, node_weight_in_ref[:width, :])
        from_gathered_ref[...] = dot_right_t(
            first_back, node_weight_in_ref[width:, :]
        ).astype(BF16)
        grads_ref[:width, :] = dot_left_t(nodes, first_back).astype(BF16)
        grads_ref[width : 2 * width, :] = dot_left_t(gathered, first_back).astype(BF16)
        grads_ref[2 * width : 3 * width, :] = dot_left_t(active, second_back).astype(BF16)
        grads_ref[3 * width :, :] = small_rows(first_wide, product, 2).astype(BF16)
        halve(grads_ref, "core", keep_ref, send_ref)


def backward_pass(
    step,
    last,
    peers,
    capacity,
    near,
    bands,
    tiles,
    count_ref,
    sender_ref,
    receiver_ref,
    edges_ref,
    cot_ref,
    active_ref,
    slope_ref,
    hat_ref,
    inverse_ref,
    table_ref,
    from_gathered_ref,
    from_node_ref,
    weight_in_ref,
    weight_out_ref,
    gain_ref,
    edge_grad_ref,
    totals_ref,
    back_far_ref,
    band_even_ref,
    band_odd_ref,
    tile_even_ref,
    tile_odd_ref,
    keep_ref,
    send_ref,
    sums_ref,
    in_sum_ref,
    out_sum_ref,
    gain_sum_ref,
    grads_ref,
    wide_ref,
    second_ref,
    first_ref,
):
    tile, width = edges_ref.shape
    node_rows = from_gathered_ref.shape[0]
    slots = table_ref.shape[0]

    @pl.when(step == 0)
    def _():
        sums_ref[...] = jnp.zeros_like(sums_ref)
        in_sum_ref[...] = jnp.zeros_like(in_sum_ref)
        out_sum_ref[...] = jnp.zeros_like(out_sum_ref)
        gain_sum_ref[...] = jnp.zeros_like(gain_sum_ref)

    sender = far_place(sender_ref[...], near, peers, capacity)
    receiver = receiver_ref[...]
    halves = strips(tile)
    for strip in halves:
        hot = lane_hot(spread_index(receiver[:, strip]), node_rows)
        wide_ref[strip, :] = dot(hot, from_gathered_ref[...])

    def normalize(strip):
        gain_sum = gain_sum_ref[...]
        for rows in chunks(strip):
            place = lax.broadcasted_iota(jnp.int32, (CHUNK, 1), 0) + (step * tile + rows.start)
            cot = cot_ref[rows, :].astype(F32) + wide_ref[rows, :]
            cot = jnp.where(place < count_ref[0], cot, 0.0)
            hat = hat_ref[rows, :].astype(F32)
            back, product = norm_back(cot, gain_ref[...], hat, inverse_ref[rows, 0:1])
            gain_sum += jnp.sum(product.reshape(CHUNK // 8, 8, width), axis=0)
            second_ref[rows, :] = back.astype(BF16)
        gain_sum_ref[...] = gain_sum
        wide_ref[strip, :] = dot_right_t(second_ref[strip, :], weight_out_ref[...])

    def activate(strip):
        for rows in chunks(strip):
            first_ref[rows, :] = (wide_ref[rows, :] * slope_ref[rows, :].astype(F32)).astype(BF16)
        wide_ref[strip, :] = dot_right_t(first_ref[strip, :], weight_in_ref[:width, :])

    for work in (normalize, activate):
        for strip in halves:
            work(strip)
    out_sum_ref[...] += dot_left_t(active_ref[...], second_ref[...])
    for rows in chunks(slice(0, tile)):
        edge_grad_ref[rows, :] = (cot_ref[rows, :].astype(F32) + wide_ref[rows, :]).astype(BF16)
    first_back = first_ref[...]
    in_sum_ref[...] += dot_left_t(edges_ref[...], first_back)
    sums_ref[:slots, :] += dot(sublane_hot(sender, slots), first_back)
    sums_ref[slots:, :] += dot(sublane_hot(receiver, node_rows), first_back)

    @pl.when(step == last)
    def _():
        sent = sums_ref[:slots, :].astype(BF16)
        received_wide = sums_ref[slots:, :]
        received = received_wide.astype(BF16)
        grads_ref[:width, :] = in_sum_ref[...].astype(BF16)
        grads_ref[width : 2 * width, :] = dot_left_t(table_ref[...], sent).astype(BF16)
        grads_ref[2 * width : 3 * width, :] = dot_left_t(
            table_ref[:node_rows, :], received
        ).astype(BF16)
        grads_ref[3 * width : 4 * width, :] = out_sum_ref[...].astype(BF16)
        grads_ref[4 * width :, :] = small_rows(received_wide, gain_sum_ref[...], 0).astype(BF16)
        halve(grads_ref, "core", keep_ref, send_ref)
        sent_back = dot_right_t(sent, weight_in_ref[width : 2 * width, :])
        totals_ref[...] = (
            from_node_ref[...]
            + dot_right_t(received, weight_in_ref[2 * width :, :])
            + sent_back[:node_rows, :]
        )
        place = node_rows
        rims = (band_even_ref, band_odd_ref, tile_even_ref, tile_odd_ref)
        for number, rim in enumerate(rims):
            axes, first = ((bands, place), (tiles, place + 2 * rim.shape[0]))[number // 2]
            before = sent_back[first : first + rim.shape[0], :]
            after = sent_back[first + rim.shape[0] : first + 2 * rim.shape[0], :]
            rim[...] = jnp.where(towards(axes, number % 2) == 1, after, before).astype(BF16)
        place += 4 * rims[0].shape[0]
        for slot in range(capacity):
            spread_rows(back_far_ref, slot, sent_back[place : place + peers, :])
            place += peers


def passes_kernel(peers, capacity, near, bands, tiles, *refs):
    ins, outs, scratch = refs[:20], refs[20:31], refs[31:]
    count, sender, receiver, edges, cot = ins[:5]
    nodes, *halo, weight_in, bias, weight_out, gain = ins[5:15]
    edge_out, edge_grad, node_out, totals, back_far, *back_rims, keep, send = outs
    active, slope, hat, inverse, table, from_gathered, from_node = scratch[:7]
    projected, gathered, grads, hot, wide, second, first, sums, in_sum, out_sum, gain_sum = scratch[7:]
    tile, width = edges.shape
    steps = pl.num_programs(0) // 2
    step = lax.rem(pl.program_id(0), steps)
    rows = pl.ds(pl.multiple_of(step * tile, tile), tile)
    saved = [ref.at[rows, :] for ref in (active, slope, hat, inverse)]
    node_half = 3 * width // 2 + SMALL
    node_ends = [ref.at[:node_half, :] for ref in (keep, send)]
    edge_ends = [ref.at[node_half:, :] for ref in (keep, send)]

    @pl.when(pl.program_id(0) < steps)
    def _():
        forward_pass(
            step,
            steps - 1,
            peers,
            capacity,
            bands,
            tiles,
            count,
            sender,
            receiver,
            edges,
            nodes,
            *halo,
            weight_in,
            bias,
            weight_out,
            gain,
            *ins[15:],
            edge_out,
            *saved,
            table,
            node_out,
            from_gathered,
            from_node,
            *node_ends,
            projected,
            gathered,
            grads.at[: 3 * width + SMALL, :],
            hot,
            wide,
            second,
        )

    @pl.when(pl.program_id(0) >= steps)
    def _():
        backward_pass(
            step,
            steps - 1,
            peers,
            capacity,
            near,
            bands,
            tiles,
            count,
            sender,
            receiver,
            edges,
            cot,
            *saved,
            table,
            from_gathered,
            from_node,
            weight_in,
            weight_out,
            gain,
            edge_grad,
            totals,
            back_far,
            *back_rims,
            *edge_ends,
            sums,
            in_sum,
            out_sum,
            gain_sum,
            grads,
            wide,
            second,
            first,
        )


def return_kernel(bands, tiles, halo_ref, far_ref, totals_ref, returned_ref, *refs):
    rims, out_ref = refs[:-1], refs[-1]
    count, width = totals_ref.shape
    capacity, peers = far_ref.shape[1:]
    total = totals_ref[...]
    for number, rim in enumerate(rims):
        axes, first = ((bands, 0), (tiles, 2))[number // 2]
        chosen = halo_ref[0, first : first + 1, :]
        after = halo_ref[0, first + 1 : first + 2, :]
        chosen = jnp.where(towards(axes, number % 2) == 1, after, chosen)
        total += dot(sublane_hot(chosen, count), rim[...])
    for slot in range(capacity):
        hot = sublane_hot(far_ref[0, slot : slot + 1, :], count)
        total += dot(hot, block_rows(returned_ref, slot, peers, width).astype(BF16))
    out_ref[...] = total.astype(BF16)


def swap(array, axes, step, wrap):
    size = lax.axis_size(axes)
    pairs = []
    for low in range(step, size if wrap else size - 1, 2):
        high = (low + 1) % size
        pairs += [(low, high), (high, low)]
    return lax.ppermute(array, axes, pairs)


def after(arrays, *others):
    return lax.optimization_barrier((arrays, others))[0]


def limits(megabytes=62):
    return pltpu.CompilerParams(
        dimension_semantics=("arbitrary",), vmem_limit_bytes=megabytes * 2**20
    )


def shards(
    x_axes,
    y_axes,
    node_latents,
    edge_latents,
    edge_count,
    receiver,
    sender,
    halo_send,
    far_send,
    edge_weight_in,
    edge_bias,
    edge_weight_out,
    edge_gain,
    node_weight_in,
    node_bias,
    node_weight_out,
    node_gain,
    cot_nodes,
    cot_edges,
):
    node_rows, width = node_latents.shape
    edge_rows = edge_latents.shape[0]
    border = halo_send.shape[2]
    peers = far_send.shape[1]
    capacity = far_send.shape[2]
    rims = 4 * border
    fars = peers * capacity
    used = node_rows + rims + fars
    slots = -(-used // LANES) * LANES
    tile = TILE
    steps = edge_rows // tile

    far_send = jnp.swapaxes(far_send, 1, 2)
    sender = sender.reshape(1, edge_rows)
    receiver = receiver.reshape(1, edge_rows)
    bands = (*x_axes, "core")
    tiles = ("z", *y_axes)
    everyone = bands + tiles

    def exchanged(blocks):
        parts = blocks.reshape(peers, -1, LANES)
        return lax.all_to_all(parts, everyone, split_axis=0, concat_axis=0, tiled=True).reshape(
            -1, LANES
        )

    def call(kernel, name, out_shape, *args, scratch=()):
        return pl.pallas_call(
            kernel,
            out_shape=out_shape,
            scratch_shapes=scratch,
            compiler_params=pltpu.CompilerParams(vmem_limit_bytes=62 * 2**20),
            name=name,
        )(*args)

    def packed(*shape):
        return jax.ShapeDtypeStruct(shape, BF16)

    def wide(*shape):
        return jax.ShapeDtypeStruct(shape, F32)

    def across(array, axes):
        last = 2 ** len(axes) - 1
        return lax.ppermute(array, axes, [(i, last - i) for i in range(last + 1)])

    def ahead(array, step):
        size = lax.axis_size("z")
        return lax.ppermute(array, "z", [(i, (i + step) % size) for i in range(size)])

    rim_shape = jax.ShapeDtypeStruct((border, width), BF16)
    far_shape = jax.ShapeDtypeStruct((fars * width // LANES, LANES), F32)
    far_rows, *rim_rows = call(
        partial(pick_kernel, bands, tiles),
        "pick",
        (far_shape,) + (rim_shape,) * 4,
        halo_send,
        far_send,
        node_latents,
    )
    def swapped(rims):
        return [
            swap(rims[0], bands, 0, False),
            swap(rims[1], bands, 1, False),
            swap(rims[2], tiles, 0, True),
            swap(rims[3], tiles, 1, True),
        ]

    got_rims = swapped(rim_rows)
    incoming = exchanged(far_rows)

    def whole(*shape):
        return pl.BlockSpec(shape, lambda i: (0,) * len(shape))

    both = pl.BlockSpec((tile, width), lambda i: (i % steps, 0))
    ahead_only = pl.BlockSpec((tile, width), lambda i: (jnp.minimum(i, steps - 1), 0))
    back_only = pl.BlockSpec((tile, width), lambda i: (jnp.maximum(i - steps, 0), 0))
    index_spec = pl.BlockSpec((1, tile), lambda i: (0, i % steps))
    scalar = pl.BlockSpec(memory_space=pltpu.SMEM)
    rim_spec = whole(border, width)
    far_spec = whole(*far_shape.shape)
    line, node_spec, square = whole(1, width), whole(node_rows, width), whole(width, width)
    node_half = 3 * width // 2 + SMALL
    edge_half = 4 * width // 2 + SMALL
    flat = packed(edge_rows, width)
    core_half = packed(node_half + edge_half, width)
    (edge_out, edge_grad, node_out, totals, back_far, *back_rims, keep, send) = pl.pallas_call(
        partial(passes_kernel, peers, capacity, node_rows + rims, bands, tiles),
        grid=(2 * steps,),
        in_specs=[scalar, index_spec, index_spec, both, back_only, node_spec]
        + [rim_spec] * 4
        + [far_spec, whole(3 * width, width), line, square, line]
        + [whole(2 * width, width), line, square, line, node_spec],
        out_specs=(ahead_only, back_only, node_spec, node_spec, far_spec)
        + (rim_spec,) * 4
        + (whole(*core_half.shape),) * 2,
        out_shape=(flat, flat, packed(node_rows, width), wide(node_rows, width), far_shape)
        + (rim_shape,) * 4
        + (core_half,) * 2,
        scratch_shapes=[
            pltpu.VMEM((edge_rows, width), BF16),
            pltpu.VMEM((edge_rows, width), BF16),
            pltpu.VMEM((edge_rows, width), BF16),
            pltpu.VMEM((edge_rows, LANES), F32),
            pltpu.VMEM((slots, width), BF16),
            pltpu.VMEM((node_rows, width), BF16),
            pltpu.VMEM((node_rows, width), F32),
            pltpu.VMEM((slots + node_rows, width), BF16),
            pltpu.VMEM((node_rows, width), F32),
            pltpu.VMEM((4 * width + SMALL, width), BF16),
            pltpu.VMEM((tile, slots + node_rows), BF16),
            pltpu.VMEM((tile, width), F32),
            pltpu.VMEM((tile, width), BF16),
            pltpu.VMEM((tile, width), BF16),
            pltpu.VMEM((slots + node_rows, width), F32),
            pltpu.VMEM((width, width), F32),
            pltpu.VMEM((width, width), F32),
            pltpu.VMEM((8, width), F32),
        ],
        compiler_params=limits(),
        cost_estimate=pl.CostEstimate(
            flops=2 * 10**10, bytes_accessed=2 * 10**7, transcendentals=10**6
        ),
        name="passes",
    )(
        edge_count,
        sender,
        receiver,
        edge_latents,
        cot_edges,
        node_latents,
        *got_rims,
        incoming,
        edge_weight_in,
        edge_bias.reshape(1, width),
        edge_weight_out,
        edge_gain.reshape(1, width),
        node_weight_in,
        node_bias.reshape(1, width),
        node_weight_out,
        node_gain.reshape(1, width),
        cot_nodes,
    )
    core_got = across(send, ("core",))
    plane = x_axes + y_axes
    sides = [()]
    for axis in plane:
        sides += [flips + (axis,) for flips in sides]
    depth = lax.axis_size("z")
    edge_part = (edge_half - SMALL) // len(sides)
    node_part = (node_half - SMALL) // len(sides)
    part = -(-(edge_part + node_part) // (16 * depth)) * 16
    parts = call(
        partial(plane_kernel, plane, sides, node_half),
        "plane",
        (packed(part * depth + SMALL, width),) * len(sides),
        keep,
        core_got,
    )
    got = [across(array, flips) for array, flips in zip(parts[1:], sides[1:])]

    back_far, back_rims = after((back_far, back_rims), parts)
    returned_rims = swapped(back_rims)
    returned = exchanged(back_far)
    parts = call(
        partial(line_kernel, len(sides)),
        "line",
        (packed(part + SMALL, width),) * depth,
        *after((parts[0], *got), returned, returned_rims[:2]),
        scratch=[pltpu.VMEM((part * depth + SMALL, width), BF16)],
    )
    got = [ahead(parts[step], step) for step in range(1, depth)]
    own, small = call(
        total_kernel,
        "total",
        (packed(part, width), wide(SMALL, width)),
        *after((parts[0], *got), returned_rims[2:]),
    )
    lines, bit = {0: own}, depth // 2
    while bit:
        for step, piece in list(lines.items()):
            lines[step + bit] = lax.ppermute(piece, "z", [(i, i ^ bit) for i in range(depth)])
        bit //= 2
    middle = part * depth // 2
    own, top, bottom = call(
        join_kernel,
        "join",
        (packed(2 * middle, width), packed(middle, width), packed(middle, width)),
        *(lines[step] for step in range(depth)),
    )
    grad_nodes = call(
        partial(return_kernel, bands, tiles),
        "returned",
        packed(node_rows, width),
        *after((halo_send, far_send, totals, returned, *returned_rims), own),
    )

    copies = edge_part // math.gcd(edge_part, 3 * width) + node_part // math.gcd(node_part, 2 * width)
    anywhere, here = pl.BlockSpec(memory_space=pl.ANY), pl.BlockSpec(memory_space=pltpu.VMEM)
    whole_grads = (wide(3 * width, width), wide(width, width))
    whole_grads += (wide(2 * width, width), wide(width, width))

    def finished(pieces, extra):
        rows = sum(piece.shape[0] for piece in pieces.values())
        first = len(extra) == 1
        return pl.pallas_call(
            partial(finish_kernel, plane, edge_part, node_part, tuple(pieces.keys())),
            out_shape=whole_grads + (wide(width),) * (4 if first else 0),
            in_specs=[here] * len(pieces) + ([here] if first else [anywhere] * 4),
            out_specs=(anywhere,) * 4 + (here,) * (4 if first else 0),
            input_output_aliases={} if first else {len(pieces) + i: i for i in range(4)},
            scratch_shapes=[
                pltpu.VMEM((rows, width), F32),
                pltpu.SemaphoreType.DMA((copies * len(pieces),)),
            ],
            compiler_params=pltpu.CompilerParams(vmem_limit_bytes=62 * 2**20),
            name="finish",
        )(*pieces.values(), *extra)

    held = {((), 0): own}
    if len(plane) == 2:
        one, two = plane
        held[(one,), middle] = across(bottom, (one,))
        held[(two,), 0] = across(top, (two,))
        held[(one,), 0] = across(top, (one,))
        held[(two,), middle] = across(bottom, (two,))
        late = {
            (plane, 0): across(held[(two,), 0], (one,)),
            (plane, middle): across(held[(one,), middle], (two,)),
        }
        for flips in ((one,), (two,)):
            for first in (0, middle):
                late[flips + ("core",), first] = across(held[flips, first], ("core",))
        held[("core",), 0] = across(own, ("core",))
        *grads, bias, gain, node_small, node_scale = finished(held, (after(small, grad_nodes),))
        for first in (0, middle):
            piece = after(late[plane, first], bias)
            late[plane + ("core",), first] = across(piece, ("core",))
    else:
        for flips in sides[1:]:
            held[flips, 0] = across(own, flips)
        late = {
            (flips + ("core",), first): across(piece, ("core",))
            for (flips, first), piece in held.items()
        }
        *grads, bias, gain, node_small, node_scale = finished(held, (small,))
    grads = finished(late, grads)
    return (
        node_out,
        edge_out,
        grad_nodes,
        edge_grad,
        grads[0],
        bias,
        grads[1],
        gain,
        grads[2],
        node_small,
        grads[3],
        node_scale,
    )


def solution(mesh):
    bands, tiles = mesh.devices.shape
    x_axes = tuple(f"x{bit}" for bit in range((bands // 2).bit_length() - 1))
    y_axes = tuple(f"y{bit}" for bit in range((tiles.bit_length() - 1) // 2))
    names = (*x_axes, "core", "z", *y_axes)
    shape = (2,) * len(x_axes) + (2, tiles // 2 ** len(y_axes)) + (2,) * len(y_axes)
    cores = jax.sharding.Mesh(mesh.devices.reshape(shape), names)
    spread = P(names, None)
    line = P(names)
    cube = P(names, None, None)
    return jax.shard_map(
        partial(shards, x_axes, y_axes),
        mesh=cores,
        in_specs=(spread, spread, line, line, line, cube, cube) + (P(),) * 8 + (spread, spread),
        out_specs=(spread, spread, spread, spread) + (P(),) * 8,
        check_vma=False,
    )
```
